32 devices in a mesh: orb: 32 (over z, y, x, core).
Axes of the slice: x: 2, y: 2, z: 4, core: 2. Of those that a mesh axis runs over, the one named last changes fastest.
Arguments:
- slabs: float32 [64, 384, 768], P('orb'), may hold values from -1.2 to 1.2
- amplitudes: float32 [256, 384, 384], P('orb'), may hold values from -6 to 6
- intersections: float32 [256, 3, 384, 384], P('orb'), may hold values from -0.3125 to 0.3125
- fock_coupling: float32 [256, 3], P('orb'), may hold values from -0.9 to 0.9
- virt_energy: float32 [256, 384], P('orb'), may hold values from 0.4 to 4
- occ_pair_energy: float32 [256], P('orb'), may hold values from -2.4 to -0.4
- pair_orbs: int32 [256, 2], P('orb'), may hold values from 0 to 63, as said below
- couplings: int32 [256, 3], P('orb'), may hold values from 0 to 255, as said below
Outputs:
- updated_amplitudes: float32 [256, 384, 384], P('orb')
The draws below stay inside these ranges and needn't reach their ends.
Inputs may be any that keep to these rules, and one draw needn't show every extreme that they name: `pair_orbs`: row p holds orbitals (i, j), i != j. A device's block of 8 rows has i among that device's own 2 orbitals (rows of its block of slabs) and j among the orbitals of a device at most 2 away along the axis, counted without wrapping (the first and last devices are not neighbours here); every device's block names orbitals of some device 2 away and of some device next to it. `couplings`: entry (p, c) is a pair coupled to pair p. For c = 0 it is a pair in the block of the device before p's owner, and for c = 1 a pair in the block of the device after it. The axis closes: before the first device comes the last one, and after the last comes the first. Over one device's block of 8 rows, column 0 names exactly 4 distinct pairs, and so does column 1. For c = 2 it is another pair of p's own block.
All inputs are finite; a program needn't handle non-finite values.
Results may differ from the reference program's by a relative error of at most 0.0001.
Values sent between devices are 32-bit elements; how exact they have to be, the bound alone decides.
No kernel may reach another device: no remote copies, remote signals or barrier semaphores. Data moves between devices by JAX's collectives and lax.ppermute only.
A program may use at most 192 MiB of HBM per device.

```python
import math
import jax
import jax.numpy as jnp
from jax import lax

NV = 384
NQ = 768
O_DEV = 2
P_DEV = 8
COUP = 3
REACH = 2
ITERS = 2
NOCC = 64
PAIRS = 256


def draw_pair_orbs(key, part):
    device_count = PAIRS // P_DEV
    keys = jax.random.split(jax.random.fold_in(key, 101), 5)
    device = jnp.arange(device_count, dtype=jnp.int32)[:, None]
    slot = jnp.arange(P_DEV, dtype=jnp.int32)[None, :]
    fixed_offsets = jnp.array([-REACH, REACH, -1, 1], jnp.int32)
    shape = (device_count, P_DEV)
    magnitude = jax.random.randint(keys[0], shape, 1, REACH + 1)
    direction = 2 * jax.random.randint(keys[1], shape, 0, 2) - 1
    base = jnp.where(slot < 4, fixed_offsets[jnp.minimum(slot, 3)], magnitude * direction)
    scores = jax.random.randint(keys[2], shape, 0, 1 << 20) * P_DEV + slot
    order = jnp.argsort(scores, axis=1)
    offsets = jnp.take_along_axis(base, order, axis=1)
    target = device + offsets
    target = jnp.where((target < 0) | (target >= device_count), device - offsets, target)
    first = device * O_DEV + jax.random.randint(keys[3], shape, 0, O_DEV)
    second = target * O_DEV + jax.random.randint(keys[4], shape, 0, O_DEV)
    return jnp.stack([first, second], axis=-1).reshape(PAIRS, 2).astype(jnp.int32)


def draw_couplings(key, part):
    device_count = PAIRS // P_DEV
    half_count = P_DEV // 2
    keys = jax.random.split(jax.random.fold_in(key, 202), 3)
    device = jnp.arange(device_count, dtype=jnp.int32)[:, None, None]
    slot = jnp.arange(P_DEV, dtype=jnp.int32)[None, :, None]
    column = jnp.arange(COUP, dtype=jnp.int32)[None, None, :]
    side = jnp.where(column == 0, -1, jnp.where(column == 1, 1, 0))
    target = (device + side) % device_count
    subset_scores = jax.random.randint(keys[0], (device_count, COUP, P_DEV), 0, 1 << 20) * P_DEV + jnp.arange(P_DEV, dtype=jnp.int32)
    subset = jnp.argsort(subset_scores, axis=2).astype(jnp.int32)
    pick_scores = jax.random.randint(keys[1], (device_count, COUP, P_DEV), 0, 1 << 20) * P_DEV + jnp.arange(P_DEV, dtype=jnp.int32)
    pick_order = (jnp.argsort(pick_scores, axis=2) % half_count).astype(jnp.int32)
    chosen = jnp.take_along_axis(subset, pick_order, axis=2)
    chosen = jnp.transpose(chosen, (0, 2, 1))
    other = (slot + 1 + jax.random.randint(keys[2], (device_count, P_DEV, COUP), 0, P_DEV - 1)) % P_DEV
    within = jnp.where(side == 0, other, chosen)
    return (target * P_DEV + within).reshape(PAIRS, COUP).astype(jnp.int32)


def block_scale(stream_key, dims, shards, least, largest):
    gain = 1.0
    for dim, shards_of in shards:
        steps = jax.random.uniform(jax.random.fold_in(jax.random.fold_in(stream_key, 6), dim), (shards_of,), jnp.float32, least / len(shards), largest / len(shards))
        gain = gain * jnp.repeat(jnp.exp(steps), dims[dim] // shards_of).reshape((-1,) + (1,) * (len(dims) - 1 - dim))
    return gain


def centred(rng, shape, deviation, reach, cuts=(), held_as=jnp.bfloat16):
    values = deviation * jax.random.normal(rng, shape, jnp.float32)
    if cuts:
        values = values * block_scale(rng, shape, cuts, -0.22, 0.18)
    return jnp.clip(values, -reach, reach).astype(held_as)


def setup_inputs(seed: int = 0) -> dict:
    seeds = jax.random.split(jax.random.key(seed), 9)
    return {
        "slabs": centred(seeds[0], (NOCC, NV, NQ), 0.19, 1.2, ((0, 32),), jnp.float32),
        "amplitudes": centred(seeds[1], (PAIRS, NV, NV), 1.0, 6.0, ((0, 32),), jnp.float32),
        "intersections": centred(seeds[2], (PAIRS, COUP, NV, NV), NV ** -0.5, 0.3125, ((0, 32),), jnp.float32),
        "fock_coupling": jnp.clip(jax.random.uniform(seeds[3], (PAIRS, COUP), jnp.float32, -0.9, 0.9) * block_scale(seeds[3], (PAIRS, COUP), ((0, 32),), -0.4, 0.0), -0.9, 0.9),
        "virt_energy": jnp.clip(jnp.exp(math.log(4.0) - 2.3025851 * jax.random.uniform(seeds[4], (PAIRS, NV), jnp.float32) ** block_scale(seeds[4], (PAIRS, NV), ((0, 32),), -0.2, 0.2)), 0.4, 4.0),
        "occ_pair_energy": jnp.clip(-2.4 + 2 * jax.random.uniform(seeds[5], (PAIRS,), jnp.float32) ** block_scale(seeds[5], (PAIRS,), ((0, 32),), -0.2, 0.2), -2.4, -0.4),
        "pair_orbs": draw_pair_orbs(jax.random.fold_in(seeds[8], 71), 0),
        "couplings": draw_couplings(jax.random.fold_in(seeds[8], 71), 0),
    }


highest = lax.Precision.HIGHEST


def pair_integrals(slabs, pair_orbs):
    def one_pair(pair):
        left = slabs[pair[0]]
        right = slabs[pair[1]]
        return jnp.dot(left, right.T, precision=highest, preferred_element_type=jnp.float32)

    return lax.map(one_pair, pair_orbs)


def reference(slabs, amplitudes, intersections, fock_coupling, virt_energy, occ_pair_energy, pair_orbs, couplings):
    integrals = pair_integrals(slabs, pair_orbs)
    current = amplitudes
    for step in range(ITERS):
        def update(row):
            coupled_rows, gains, intersection, integral, virtual, occupied, own = row
            coupled = jnp.zeros((NV, NV), jnp.float32)
            for column in range(COUP):
                picked = current[coupled_rows[column]]
                half = jnp.dot(intersection[column], picked, precision=highest, preferred_element_type=jnp.float32)
                coupled = coupled + gains[column] * jnp.dot(half, intersection[column].T, precision=highest, preferred_element_type=jnp.float32)
            denominator = virtual[:, None] + virtual[None, :] - occupied
            residual = integral + denominator * own - coupled
            return own - residual / denominator

        current = lax.map(update, (couplings, fock_coupling, intersections, integrals, virt_energy, occ_pair_energy, current))
    return current
```

```python
import functools

import jax
import jax.numpy as jnp
from jax import lax
from jax.experimental import pallas as pl
from jax.experimental.pallas import tpu as pltpu
from jax.sharding import PartitionSpec as P

REACH = 2
ITERS = 2
CHUNKS = 3

f32 = jnp.float32
bf16 = jnp.bfloat16
ANY = pl.BlockSpec(memory_space=pl.ANY)
SMEM = pl.BlockSpec(memory_space=pltpu.SMEM)
VMEM = pl.BlockSpec(memory_space=pltpu.VMEM)
PARAMS = pltpu.CompilerParams(vmem_limit_bytes=63 * 1024 * 1024)

INTRA, CROSS, ORDER, START, SEND_INTRA, SEND_CROSS, EARLY, EARLY_COUNT, LEFT, RIGHT, COLUMN, SECTIONS = range(12)


def after(value, *earlier):
    return lax.optimization_barrier((value,) + earlier)[0]


def cost(flops, moved):
    return pl.CostEstimate(flops=flops // 1000, bytes_accessed=moved // 1000, transcendentals=0)


def split(x):
    hi = x.astype(bf16)
    lo = (x - hi.astype(f32)).astype(bf16)
    return hi, lo


def dot_nn(a, b):
    return lax.dot_general(a, b, (((1,), (0,)), ((), ())), preferred_element_type=f32)


def dot_nt(a, b):
    return lax.dot_general(a, b, (((1,), (1,)), ((), ())), preferred_element_type=f32)


def project(x, t, gain):
    nv = x.shape[0]
    xh, xl = split(x)
    th, tl = split(t)
    wide = dot_nn(xh, jnp.concatenate([th, tl], axis=1))
    half = wide[:, :nv] + wide[:, nv:] + dot_nn(xl, th)
    hh, hl = split(half * gain)
    wide = dot_nt(hh, jnp.concatenate([xh, xl], axis=0))
    return wide[:, :nv] + wide[:, nv:] + dot_nt(hl, xh)


def plan_kernel(devices, orbitals, where, couplings, lists_intra, lists_cross, pair_orbs, plan, seen):
    pairs = couplings.shape[0]
    half = pairs // 2
    device = where[0]
    core = device % 2
    odd = (device // 2) % 2
    partner = device + 1 - 2 * core
    outside = (device - 1 + 2 * core + devices) % devices

    def mark(lists, column, base):
        for q in range(pairs):
            seen[q] = 0
        for p in range(pairs):
            seen[lists[p, column] - base] = 1

    def ranks(lists, column, base, section):
        mark(lists, column, base)
        below = jnp.int32(0)
        for q in range(pairs):
            here = seen[q]
            seen[q] = below
            below = below + here
        for p in range(pairs):
            plan[section * pairs + p] = jnp.minimum(seen[lists[p, column] - base], half - 1)

    def sends(lists, column, section):
        mark(lists, column, device * pairs)
        below = jnp.int32(0)
        for q in range(pairs):
            here = seen[q]
            plan[section * pairs + q] = jnp.where(jnp.logical_and(here == 1, below < half), below, -1)
            below = below + here

    def sort(section, key, keys, cuts):
        filled = jnp.int32(0)
        for k in range(keys):
            if cuts is not None:
                plan[cuts * pairs + k] = filled
            for p in range(pairs):
                mine = key(p) == k

                @pl.when(mine)
                def _():
                    plan[section * pairs + filled] = p

                filled = filled + mine.astype(jnp.int32)
        if cuts is not None:
            plan[cuts * pairs + keys] = filled

    ranks(couplings, 1 - core, partner * pairs, INTRA)
    ranks(couplings, core, outside * pairs, CROSS)
    sends(lists_intra, core, SEND_INTRA)
    sends(lists_cross, 1 - core, SEND_CROSS)
    sort(ORDER, lambda p: plan[CROSS * pairs + p], half, START)

    swapped = (REACH + 1 - 2 * core) * orbitals
    near = (1 - odd) * 2 * REACH * orbitals
    late = jnp.int32(0)
    for p in range(pairs):
        right = pair_orbs[p, 1] - (device - REACH) * orbitals
        plan[LEFT * pairs + p] = pair_orbs[p, 0] - device * orbitals
        plan[RIGHT * pairs + p] = right
        first = jnp.logical_or(
            jnp.logical_and(right >= swapped, right < swapped + orbitals),
            jnp.logical_and(right >= near, right < near + orbitals),
        )
        seen[p] = 1 - first.astype(jnp.int32)
        late = late + seen[p]
    sort(EARLY, lambda p: seen[p], 2, None)
    plan[EARLY_COUNT * pairs] = pairs - late
    plan[COLUMN * pairs] = 1 - core
    plan[COLUMN * pairs + 1] = core
    plan[COLUMN * pairs + 2] = swapped
    plan[COLUMN * pairs + 3] = near
    plan[COLUMN * pairs + 4] = 2 * REACH * orbitals - near
    plan[COLUMN * pairs + 5] = 2 * REACH * orbitals - swapped


def make_plan(devices, orbitals, where, couplings, lists_intra, lists_cross, pair_orbs):
    pairs = couplings.shape[0]
    return pl.pallas_call(
        functools.partial(plan_kernel, devices, orbitals),
        out_shape=jax.ShapeDtypeStruct((SECTIONS * pairs,), jnp.int32),
        in_specs=[SMEM] * 5,
        out_specs=SMEM,
        scratch_shapes=[pltpu.SMEM((pairs,), jnp.int32)],
        name="plan",
    )(where, couplings, lists_intra, lists_cross, pair_orbs)


def send_copies(p, plan, source, cross, intra, cross_sem, intra_sem, act):
    pairs = plan.shape[0] // SECTIONS
    for section, outs, sem in ((SEND_CROSS, cross, cross_sem), (SEND_INTRA, intra, intra_sem)):
        place = plan[section * pairs + p]
        for r, out in enumerate(outs):

            @pl.when(place == r)
            def _():
                act(pltpu.make_async_copy(source, out, sem.at[r]))


def start(copy):
    copy.start()


def wait(copy):
    copy.wait()


def rank_groups(half):
    return [(0, half - 1), (half - 1, half)]


def send_shapes(half, nv):
    sizes = [high - low for low, high in rank_groups(half)] + [half]
    return [jax.ShapeDtypeStruct((size, nv, nv), f32) for size in sizes]


def send_views(half, outs):
    groups = rank_groups(half)
    cross = [outs[k].at[r] for k, (low, high) in enumerate(groups) for r in range(high - low)]
    return cross, [outs[len(groups)].at[r] for r in range(half)]


def gather_kernel(plan, current, *rest):
    outs, (rows, load_sem, cross_sem, intra_sem) = rest[:-4], rest[-4:]
    pairs = current.shape[0]
    half = pairs // 2
    cross, intra = send_views(half, outs)
    loads = [pltpu.make_async_copy(current.at[p], rows.at[p], load_sem.at[p]) for p in range(pairs)]
    for load in loads:
        load.start()
    for p in range(pairs):
        loads[p].wait()
        send_copies(p, plan, rows.at[p], cross, intra, cross_sem, intra_sem, start)
    for p in range(pairs):
        send_copies(p, plan, rows.at[p], cross, intra, cross_sem, intra_sem, wait)


def gather_rows(plan, current):
    pairs, nv, _ = current.shape
    half = pairs // 2
    outs = pl.pallas_call(
        gather_kernel,
        out_shape=send_shapes(half, nv),
        in_specs=[SMEM, ANY],
        out_specs=[ANY] * len(send_shapes(half, nv)),
        scratch_shapes=[
            pltpu.VMEM((pairs, nv, nv), f32),
            pltpu.SemaphoreType.DMA((pairs,)),
            pltpu.SemaphoreType.DMA((half,)),
            pltpu.SemaphoreType.DMA((half,)),
        ],
        compiler_params=PARAMS,
        cost_estimate=cost(0, 2 * pairs * nv * nv * 4),
        name="gather_rows",
    )(plan, current)
    return list(outs[:-1]), outs[-1]


def couple_kernel(column, plan, x, t, gain, *rest):
    p = pl.program_id(0)
    c = column if column is not None else plan[COLUMN * pl.num_programs(0)]
    value = project(x[0, 0], t[0], gain[p, c])
    rest[-1][0] = value if len(rest) == 1 else rest[0][0] + value


def couple(column, section, plan, x, t, gain, before=None):
    pairs, _, nv, _ = x.shape
    square = pl.BlockSpec((1, nv, nv), lambda p, plan: (p, 0, 0))
    which = lambda plan: column if column is not None else plan[COLUMN * pairs]
    in_specs = [
        pl.BlockSpec((1, 1, nv, nv), lambda p, plan: (p, which(plan), 0, 0)),
        pl.BlockSpec((1, nv, nv), lambda p, plan: (plan[section * pairs + p], 0, 0)),
        SMEM,
    ]
    operands = [x, t, gain]
    if before is not None:
        in_specs.append(square)
        operands.append(before)
    return pl.pallas_call(
        functools.partial(couple_kernel, column),
        out_shape=jax.ShapeDtypeStruct((pairs, nv, nv), f32),
        grid_spec=pltpu.PrefetchScalarGridSpec(
            num_scalar_prefetch=1, grid=(pairs,), in_specs=in_specs, out_specs=square
        ),
        compiler_params=PARAMS,
        cost_estimate=cost(pairs * 12 * nv**3, pairs * nv * nv * 12),
        name="couple",
    )(plan, *operands)


def finish_kernel(low, high, sending, plan, gain, occ, across, down, x, before, integral, own, *rest):
    rest, scratch = rest[:-12], rest[-12:]
    x_buf, t_buf, before_buf, integral_buf, own_buf, out_buf, sem, t_sem, out_sem, cross_sem, intra_sem, _ = scratch
    pairs = x.shape[0]
    half = pairs // 2
    t = rest[0]
    outs = rest[len(rest) - (len(rank_groups(half)) + 2 if sending else 1) :]
    out = outs[0]
    first = plan[START * pairs + low]
    count = plan[START * pairs + high] - first
    column = plan[COLUMN * pairs + 1]
    pair = lambda s: plan[ORDER * pairs + first + s]

    def fetch(s, slot):
        p = pair(s)
        return (
            pltpu.make_async_copy(x.at[p, column], x_buf.at[slot], sem.at[slot, 0]),
            pltpu.make_async_copy(before.at[p], before_buf.at[slot], sem.at[slot, 1]),
            pltpu.make_async_copy(integral.at[p], integral_buf.at[slot], sem.at[slot, 2]),
            pltpu.make_async_copy(own.at[p], own_buf.at[slot], sem.at[slot, 3]),
        )

    def stores(s, act):
        p = pair(s)
        act(pltpu.make_async_copy(out_buf.at[s], out.at[p], out_sem.at[s]))
        if sending:
            cross, intra = send_views(half, outs[1:])
            send_copies(p, plan, out_buf.at[s], cross, intra, cross_sem, intra_sem, act)

    t_copies = [pltpu.make_async_copy(t.at[k], t_buf.at[k], t_sem.at[k]) for k in range(high - low)]

    @pl.when(count > 0)
    def _():
        for copy in fetch(0, 0):
            copy.start()

    for copy in t_copies:
        copy.start()
    for copy in t_copies:
        copy.wait()

    def one(s, carry):
        slot = s % 2

        @pl.when(s + 1 < count)
        def _():
            for copy in fetch(s + 1, 1 - slot):
                copy.start()

        for copy in fetch(s, slot):
            copy.wait()
        p = pair(s)
        picked = t_buf[plan[CROSS * pairs + p] - low]
        coupled = before_buf[slot] + project(x_buf[slot], picked, gain[p, column])
        lane = lax.broadcasted_iota(jnp.int32, down.shape, 1)
        tall = jnp.sum(jnp.where(lane == p, down[...], 0.0), axis=1, keepdims=True)
        denominator = tall + across[pl.ds(p, 1), :] - occ[p]
        mine = own_buf[slot]
        residual = integral_buf[slot] + denominator * mine - coupled
        out_buf[s] = mine - residual / denominator
        stores(s, start)
        return carry

    lax.fori_loop(0, count, one, 0)

    def end(s, carry):
        stores(s, wait)
        return carry

    lax.fori_loop(0, count, end, 0)


def finish(low, high, sending, plan, x, t, gain, before, integral, own, across, down, occ, done):
    pairs, _, nv, _ = x.shape
    half = pairs // 2
    operands = [plan, gain, occ, across, down, x, before, integral, own, t]
    in_specs = [SMEM] * 3 + [VMEM] * 2 + [ANY] * 5
    out_shape = [jax.ShapeDtypeStruct((pairs, nv, nv), f32)]
    if sending:
        out_shape += send_shapes(half, nv)
    aliases = {}
    if done is not None:
        aliases = {len(operands) + k: k for k in range(len(done))}
        in_specs += [ANY] * len(done)
        operands += done
    two = pltpu.VMEM((2, nv, nv), f32)
    return pl.pallas_call(
        functools.partial(finish_kernel, low, high, sending),
        out_shape=out_shape,
        in_specs=in_specs,
        out_specs=[ANY] * len(out_shape),
        scratch_shapes=[
            two,
            pltpu.VMEM((high - low, nv, nv), f32),
            two,
            two,
            two,
            pltpu.VMEM((pairs, nv, nv), f32),
            pltpu.SemaphoreType.DMA((2, 4)),
            pltpu.SemaphoreType.DMA((high - low,)),
            pltpu.SemaphoreType.DMA((pairs,)),
            pltpu.SemaphoreType.DMA((half,)),
            pltpu.SemaphoreType.DMA((half,)),
            pltpu.SMEM((1,), jnp.int32),
        ],
        input_output_aliases=aliases,
        compiler_params=PARAMS,
        cost_estimate=cost(2 * (high - low) * 12 * nv**3, 2 * (high - low) * nv * nv * 24),
        name="finish",
    )(*operands)


def integrals_kernel(early, wholes, pieces, plan, slabs, *rest):
    rest, (left_buf, high, low, right_buf, out_buf, left_sem, right_sem, out_sem) = rest[:-8], rest[-8:]
    out = rest[-1]
    orbitals, nv, nq = slabs.shape
    pairs = out.shape[0]
    per = pieces
    rows = nv // per
    bases = plan[COLUMN * pairs + 2], plan[COLUMN * pairs + 3], plan[COLUMN * pairs + 4], plan[COLUMN * pairs + 5]
    sources = []
    if wholes:
        whole = rest[0]
        sources.append((bases[0], [[whole.at[o, pl.ds(k * rows, rows)] for k in range(per)] for o in range(orbitals)]))
    used = wholes
    for base in ((bases[1],) if early else (bases[2], bases[3])):
        refs = rest[used : used + pieces]
        used += pieces
        sources.append((base, [[refs[k].at[o] for k in range(per)] for o in range(orbitals)]))
    count = plan[EARLY_COUNT * pairs] if early else pairs - plan[EARLY_COUNT * pairs]
    first = 0 if early else plan[EARLY_COUNT * pairs]
    pair = lambda s: plan[EARLY * pairs + first + s]

    def fetch(s, slot):
        right = plan[RIGHT * pairs + pair(s)]
        for base, held in sources:
            for o in range(orbitals):

                @pl.when(right == base + o)
                def _():
                    for k in range(per):
                        target = right_buf.at[slot, pl.ds(k * rows, rows)]
                        pltpu.make_async_copy(held[o][k], target, right_sem.at[slot, k]).start()

    def arrived(slot):
        for k in range(per):
            target = right_buf.at[slot, pl.ds(k * rows, rows)]
            pltpu.make_async_copy(slabs.at[0, pl.ds(k * rows, rows)], target, right_sem.at[slot, k]).wait()

    def store(s, slot):
        return pltpu.make_async_copy(out_buf.at[slot], out.at[pair(s)], out_sem.at[slot])

    lefts = [pltpu.make_async_copy(slabs.at[o], left_buf.at[o], left_sem.at[o]) for o in range(orbitals)]
    for copy in lefts:
        copy.start()

    @pl.when(count > 0)
    def _():
        fetch(0, 0)

    for o in range(orbitals):
        lefts[o].wait()
        high[o], low[o] = split(left_buf[o])

    def one(s, carry):
        slot = s % 2

        @pl.when(s + 1 < count)
        def _():
            fetch(s + 1, 1 - slot)

        arrived(slot)

        @pl.when(s >= 2)
        def _():
            store(s - 2, slot).wait()

        left = plan[LEFT * pairs + pair(s)]
        rh, rl = split(right_buf[slot])
        wide = dot_nt(high[left], jnp.concatenate([rh, rl], axis=0))
        out_buf[slot] = wide[:, :nv] + wide[:, nv:] + dot_nt(low[left], rh)
        store(s, slot).start()
        return carry

    lax.fori_loop(0, count, one, 0)

    @pl.when(count >= 2)
    def _():
        store(count - 2, count % 2).wait()

    @pl.when(count >= 1)
    def _():
        store(count - 1, (count + 1) % 2).wait()


def pair_integrals(early, plan, slabs, pairs, wholes, pieces, done=None):
    orbitals, nv, nq = slabs.shape
    operands = [plan, slabs, *wholes]
    for group in pieces:
        operands += group
    in_specs = [SMEM] + [ANY] * (len(operands) - 1)
    aliases = {}
    if done is not None:
        aliases = {len(operands): 0}
        operands.append(done)
        in_specs.append(ANY)
    return pl.pallas_call(
        functools.partial(integrals_kernel, early, len(wholes), len(pieces[0])),
        out_shape=jax.ShapeDtypeStruct((pairs, nv, nv), f32),
        in_specs=in_specs,
        out_specs=ANY,
        scratch_shapes=[
            pltpu.VMEM((orbitals, nv, nq), f32),
            pltpu.VMEM((orbitals, nv, nq), bf16),
            pltpu.VMEM((orbitals, nv, nq), bf16),
            pltpu.VMEM((2, nv, nq), f32),
            pltpu.VMEM((2, nv, nv), f32),
            pltpu.SemaphoreType.DMA((orbitals,)),
            pltpu.SemaphoreType.DMA((2, len(pieces[0]))),
            pltpu.SemaphoreType.DMA((2,)),
        ],
        input_output_aliases=aliases,
        compiler_params=PARAMS,
        cost_estimate=cost(pairs * 3 * nv * nv * nq, pairs * 2 * nv * nq),
        name="pair_integrals",
    )(*operands)


def shards(slabs, amplitudes, intersections, fock_coupling, virt_energy, occ_pair_energy, pair_orbs, couplings):
    axis = "orb"
    count = lax.axis_size(axis)
    device = lax.axis_index(axis)
    selects_near = device % 2 == (device // 2) % 2
    orbitals, nv, nq = slabs.shape
    pairs = amplitudes.shape[0]
    half = pairs // 2

    everyone = range(count)
    chip_odd = lambda i: (i // 2) % 2
    inside = [(i, i ^ 1) for i in everyone]
    beside = [(i, (i + 1) % count if i % 2 else (i - 1) % count) for i in everyone]
    near_perm = [(i, i ^ 2) for i in everyone]
    far_perm = [(i, (i - 4 if chip_odd(i) else i + 4) % count) for i in everyone]
    send = lambda value, perm: lax.ppermute(value, axis, perm)

    lists_intra = send(couplings, inside)
    lists_cross = send(couplings, beside)
    rows = nv // CHUNKS
    pieces = [slabs[:, k * rows : (k + 1) * rows] for k in range(CHUNKS)]
    *pieces, lists_intra, lists_cross = lax.optimization_barrier((*pieces, lists_intra, lists_cross))
    near = [send(piece, near_perm) for piece in pieces]

    own_row = couplings[:, 2] - device * pairs
    partial = couple(2, 0, after(own_row, *pieces), intersections, amplitudes, fock_coupling)
    near[0], partial = lax.optimization_barrier((near[0], partial))
    far = [send(near[0], far_perm)]

    where = after(device.astype(jnp.int32).reshape(1), partial)
    plan = make_plan(count, orbitals, where, couplings, lists_intra, lists_cross, pair_orbs)
    across, down = virt_energy, virt_energy.T
    cross_out, intra_out = gather_rows(plan, amplitudes)
    intra_t = send(intra_out, inside)
    slabs_swapped = send(after(slabs, intra_out), inside)

    near[1], intra_out = lax.optimization_barrier((near[1], intra_out))
    far.append(send(near[1], far_perm))
    partial = couple(None, INTRA, plan, intersections, intra_t, fock_coupling, after(partial, near[1]))
    near[2], far[0], partial, *cross_out = lax.optimization_barrier((near[2], far[0], partial, *cross_out))
    cross_t = [send(rows_out, beside) for rows_out in cross_out]
    far.append(send(near[2], far_perm))
    relayed = [send(jnp.where(selects_near, n, f), inside) for n, f in zip(near, far)]
    integrals = pair_integrals(True, plan, after(slabs, partial), pairs, [slabs_swapped], [near])
    integrals = pair_integrals(False, plan, slabs, pairs, [], [far, relayed], integrals)

    current = amplitudes
    for iteration in range(ITERS):
        if iteration > 0:
            cross_t = [send(rows_out, beside) for rows_out in cross_out]
            intra_t = send(intra_out, inside)
            partial = couple(2, 0, own_row, intersections, current, fock_coupling)
            partial = couple(None, INTRA, plan, intersections, intra_t, fock_coupling, partial)
        sending = iteration + 1 < ITERS
        done = None
        for k, (low, high) in enumerate(rank_groups(half)):
            done = finish(
                low,
                high,
                sending,
                plan,
                intersections,
                cross_t[k],
                fock_coupling,
                partial,
                integrals,
                current,
                across,
                down,
                occ_pair_energy,
                done,
            )
        current = done[0]
        if sending:
            cross_out, intra_out = done[1:-1], done[-1]
    return current


def solution(mesh):
    in_specs = (
        P("orb", None, None),
        P("orb", None, None),
        P("orb", None, None, None),
        P("orb", None),
        P("orb", None),
        P("orb"),
        P("orb", None),
        P("orb", None),
    )
    out_specs = P("orb", None, None)
    return jax.shard_map(shards, mesh=mesh, in_specs=in_specs, out_specs=out_specs, check_vma=False)
```

```python
import functools

import jax
import jax.numpy as jnp
from jax import lax
from jax.experimental import pallas as pl
from jax.experimental.pallas import tpu as pltpu
from jax.sharding import PartitionSpec as P

REACH = 2
ITERS = 2
CHUNKS = 3

f32 = jnp.float32
bf16 = jnp.bfloat16
ANY = pl.BlockSpec(memory_space=pl.ANY)
SMEM = pl.BlockSpec(memory_space=pltpu.SMEM)
VMEM = pl.BlockSpec(memory_space=pltpu.VMEM)
PARAMS = pltpu.CompilerParams(vmem_limit_bytes=63 * 1024 * 1024)

CROSS, ORDER, START, SEND, EARLY, EARLY_COUNT, LEFT, RIGHT, COLUMN, SECTIONS = range(10)


def after(value, *earlier):
    return lax.optimization_barrier((value,) + earlier)[0]


def cost(flops, moved):
    return pl.CostEstimate(flops=flops // 1000, bytes_accessed=moved // 1000, transcendentals=0)


def split(x):
    hi = x.astype(bf16)
    lo = (x - hi.astype(f32)).astype(bf16)
    return hi, lo


def dot_nn(a, b):
    return lax.dot_general(a, b, (((1,), (0,)), ((), ())), preferred_element_type=f32)


def dot_nt(a, b):
    return lax.dot_general(a, b, (((1,), (1,)), ((), ())), preferred_element_type=f32)


def project(x, t, gain):
    nv = x.shape[0]
    xh, xl = split(x)
    th, tl = split(t)
    wide = dot_nn(xh, jnp.concatenate([th, tl], axis=1))
    half = wide[:, :nv] + wide[:, nv:] + dot_nn(xl, th)
    hh, hl = split(half * gain)
    wide = dot_nt(hh, jnp.concatenate([xh, xl], axis=0))
    return wide[:, :nv] + wide[:, nv:] + dot_nt(hl, xh)


def plan_kernel(devices, orbitals, where, couplings, lists_cross, pair_orbs, plan, seen):
    pairs = couplings.shape[0]
    half = pairs // 2
    device = where[0]
    core = device % 2
    odd = (device // 2) % 2
    outside = (device - 1 + 2 * core + devices) % devices

    def mark(lists, column, base):
        for q in range(pairs):
            seen[q] = 0
        for p in range(pairs):
            seen[lists[p, column] - base] = 1

    def ranks(lists, column, base, section):
        mark(lists, column, base)
        below = jnp.int32(0)
        for q in range(pairs):
            here = seen[q]
            seen[q] = below
            below = below + here
        for p in range(pairs):
            plan[section * pairs + p] = jnp.minimum(seen[lists[p, column] - base], half - 1)

    def sends(lists, column, section):
        mark(lists, column, device * pairs)
        below = jnp.int32(0)
        for q in range(pairs):
            here = seen[q]
            plan[section * pairs + q] = jnp.where(jnp.logical_and(here == 1, below < half), below, -1)
            below = below + here

    def sort(section, key, keys, cuts):
        filled = jnp.int32(0)
        for k in range(keys):
            if cuts is not None:
                plan[cuts * pairs + k] = filled
            for p in range(pairs):
                mine = key(p) == k

                @pl.when(mine)
                def _():
                    plan[section * pairs + filled] = p

                filled = filled + mine.astype(jnp.int32)
        if cuts is not None:
            plan[cuts * pairs + keys] = filled

    ranks(couplings, core, outside * pairs, CROSS)
    sends(lists_cross, 1 - core, SEND)
    sort(ORDER, lambda p: plan[CROSS * pairs + p], half, START)

    swapped = (REACH + 1 - 2 * core) * orbitals
    near = (1 - odd) * 2 * REACH * orbitals
    late = jnp.int32(0)
    for p in range(pairs):
        right = pair_orbs[p, 1] - (device - REACH) * orbitals
        plan[LEFT * pairs + p] = pair_orbs[p, 0] - device * orbitals
        plan[RIGHT * pairs + p] = right
        first = jnp.logical_or(
            jnp.logical_and(right >= swapped, right < swapped + orbitals),
            jnp.logical_and(right >= near, right < near + orbitals),
        )
        seen[p] = 1 - first.astype(jnp.int32)
        late = late + seen[p]
    sort(EARLY, lambda p: seen[p], 2, None)
    plan[EARLY_COUNT * pairs] = pairs - late
    plan[COLUMN * pairs + 1] = core
    plan[COLUMN * pairs + 2] = swapped
    plan[COLUMN * pairs + 3] = near
    plan[COLUMN * pairs + 4] = 2 * REACH * orbitals - near
    plan[COLUMN * pairs + 5] = 2 * REACH * orbitals - swapped


def make_plan(devices, orbitals, where, couplings, lists_cross, pair_orbs):
    pairs = couplings.shape[0]
    return pl.pallas_call(
        functools.partial(plan_kernel, devices, orbitals),
        out_shape=jax.ShapeDtypeStruct((SECTIONS * pairs,), jnp.int32),
        in_specs=[SMEM] * 4,
        out_specs=SMEM,
        scratch_shapes=[pltpu.SMEM((pairs,), jnp.int32)],
        name="plan",
    )(where, couplings, lists_cross, pair_orbs)


def send_copies(p, plan, source, outs, sem, act):
    pairs = plan.shape[0] // SECTIONS
    place = plan[SEND * pairs + p]
    rank = 0
    for out in outs:
        for r in range(out.shape[0]):

            @pl.when(place == rank)
            def _():
                act(pltpu.make_async_copy(source, out.at[r], sem.at[place]))

            rank += 1


def start(copy):
    copy.start()


def wait(copy):
    copy.wait()


def rank_groups(half, iteration):
    cut = half // 2 if iteration == 0 else half - 1
    return [(0, cut), (cut, half)]


def send_shapes(half, nv, iteration):
    return [jax.ShapeDtypeStruct((high - low, nv, nv), f32) for low, high in rank_groups(half, iteration)]


def gather_kernel(plan, current, *rest):
    outs, (rows, load_sem, send_sem) = rest[:-3], rest[-3:]
    pairs = current.shape[0]
    loads = [pltpu.make_async_copy(current.at[p], rows.at[p], load_sem.at[p]) for p in range(pairs)]

    def chosen(p, act):
        @pl.when(plan[SEND * pairs + p] >= 0)
        def _():
            act(loads[p])

    for p in range(pairs):
        chosen(p, start)
    for p in range(pairs):
        chosen(p, wait)
        send_copies(p, plan, rows.at[p], outs, send_sem, start)
    for p in range(pairs):
        send_copies(p, plan, rows.at[p], outs, send_sem, wait)


def gather_rows(plan, current):
    pairs, nv, _ = current.shape
    half = pairs // 2
    shapes = send_shapes(half, nv, 0)
    return pl.pallas_call(
        gather_kernel,
        out_shape=shapes,
        in_specs=[SMEM, ANY],
        out_specs=[ANY] * len(shapes),
        scratch_shapes=[
            pltpu.VMEM((pairs, nv, nv), f32),
            pltpu.SemaphoreType.DMA((pairs,)),
            pltpu.SemaphoreType.DMA((half,)),
        ],
        compiler_params=PARAMS,
        cost_estimate=cost(0, 2 * half * nv * nv * 4),
        name="gather_rows",
    )(plan, current)


def couple_kernel(kind, low, pairs, adding, rows, x, t, gain, *rest):
    p = low + pl.program_id(0)
    value = project(x[0, 0], t[0], gain[p, rows[2 * pairs + kind]])
    rest[-1][0] = rest[0][0] + value if adding else value


def couple(kind, low, high, rows, x, t, gain, before=None, adding=False):
    pairs, _, nv, _ = x.shape
    square = pl.BlockSpec((1, nv, nv), lambda p, rows: (low + p, 0, 0))
    in_specs = [
        pl.BlockSpec((1, 1, nv, nv), lambda p, rows: (low + p, rows[2 * pairs + kind], 0, 0)),
        pl.BlockSpec((1, nv, nv), lambda p, rows: (rows[kind * pairs + low + p], 0, 0)),
        SMEM,
    ]
    operands = [x, t, gain]
    if before is not None:
        in_specs.append(square if adding else ANY)
        operands.append(before)
    return pl.pallas_call(
        functools.partial(couple_kernel, kind, low, pairs, adding),
        out_shape=jax.ShapeDtypeStruct((pairs, nv, nv), f32),
        grid_spec=pltpu.PrefetchScalarGridSpec(
            num_scalar_prefetch=1, grid=(high - low,), in_specs=in_specs, out_specs=square
        ),
        input_output_aliases={} if before is None else {4: 0},
        compiler_params=PARAMS,
        cost_estimate=cost((high - low) * 12 * nv**3, (high - low) * nv * nv * 12),
        name="couple",
    )(rows, *operands)


def finish_kernel(low, high, sending, plan, gain, occ, across, down, x, before, integral, own, *rest):
    rest, scratch = rest[:-10], rest[-10:]
    x_buf, t_buf, before_buf, integral_buf, own_buf, out_buf, sem, t_sem, out_sem, send_sem = scratch
    pairs = x.shape[0]
    t = rest[0]
    outs = rest[len(rest) - (3 if sending else 1) :]
    out = outs[0]
    first = plan[START * pairs + low]
    count = plan[START * pairs + high] - first
    column = plan[COLUMN * pairs + 1]
    pair = lambda s: plan[ORDER * pairs + first + s]

    def fetch(s, slot):
        p = pair(s)
        return (
            pltpu.make_async_copy(x.at[p, column], x_buf.at[slot], sem.at[slot, 0]),
            pltpu.make_async_copy(before.at[p], before_buf.at[slot], sem.at[slot, 1]),
            pltpu.make_async_copy(integral.at[p], integral_buf.at[slot], sem.at[slot, 2]),
            pltpu.make_async_copy(own.at[p], own_buf.at[slot], sem.at[slot, 3]),
        )

    def stores(s, act):
        p = pair(s)
        act(pltpu.make_async_copy(out_buf.at[s], out.at[p], out_sem.at[s]))
        if sending:
            send_copies(p, plan, out_buf.at[s], outs[1:], send_sem, act)

    t_copies = [pltpu.make_async_copy(t.at[k], t_buf.at[k], t_sem.at[k]) for k in range(high - low)]

    @pl.when(count > 0)
    def _():
        for copy in fetch(0, 0):
            copy.start()

    for copy in t_copies:
        copy.start()
    for copy in t_copies:
        copy.wait()

    def one(s, carry):
        slot = s % 2

        @pl.when(s + 1 < count)
        def _():
            for copy in fetch(s + 1, 1 - slot):
                copy.start()

        for copy in fetch(s, slot):
            copy.wait()
        p = pair(s)
        picked = t_buf[plan[CROSS * pairs + p] - low]
        coupled = before_buf[slot] + project(x_buf[slot], picked, gain[p, column])
        lane = lax.broadcasted_iota(jnp.int32, down.shape, 1)
        tall = jnp.sum(jnp.where(lane == p, down[...], 0.0), axis=1, keepdims=True)
        denominator = tall + across[pl.ds(p, 1), :] - occ[p]
        mine = own_buf[slot]
        residual = integral_buf[slot] + denominator * mine - coupled
        out_buf[s] = mine - residual / denominator
        stores(s, start)
        return carry

    lax.fori_loop(0, count, one, 0)

    def end(s, carry):
        stores(s, wait)
        return carry

    lax.fori_loop(0, count, end, 0)


def finish(low, high, sending, plan, x, t, gain, before, integral, own, across, down, occ, done):
    pairs, _, nv, _ = x.shape
    half = pairs // 2
    operands = [plan, gain, occ, across, down, x, before, integral, own, t]
    in_specs = [SMEM] * 3 + [VMEM] * 2 + [ANY] * 5
    out_shape = [jax.ShapeDtypeStruct((pairs, nv, nv), f32)]
    if sending:
        out_shape += send_shapes(half, nv, 1)
    aliases = {}
    if done is not None:
        aliases = {len(operands) + k: k for k in range(len(done))}
        in_specs += [ANY] * len(done)
        operands += done
    two = pltpu.VMEM((2, nv, nv), f32)
    return pl.pallas_call(
        functools.partial(finish_kernel, low, high, sending),
        out_shape=out_shape,
        in_specs=in_specs,
        out_specs=[ANY] * len(out_shape),
        scratch_shapes=[
            two,
            pltpu.VMEM((high - low, nv, nv), f32),
            two,
            two,
            two,
            pltpu.VMEM((pairs, nv, nv), f32),
            pltpu.SemaphoreType.DMA((2, 4)),
            pltpu.SemaphoreType.DMA((high - low,)),
            pltpu.SemaphoreType.DMA((pairs,)),
            pltpu.SemaphoreType.DMA((half,)),
        ],
        input_output_aliases=aliases,
        compiler_params=PARAMS,
        cost_estimate=cost(2 * (high - low) * 12 * nv**3, 2 * (high - low) * nv * nv * 24),
        name="finish",
    )(*operands)


def integrals_kernel(early, groups, plan, slabs, *rest):
    rest, (left_buf, high, low, right_buf, out_buf, left_sem, right_sem, out_sem) = rest[:-8], rest[-8:]
    out = rest[-1]
    orbitals, nv, nq = slabs.shape
    pairs = out.shape[0]
    sources, used = [], 0
    for k, pieces in enumerate(groups):
        sources.append((plan[COLUMN * pairs + (2 if early else 4) + k], rest[used : used + pieces]))
        used += pieces
    count = plan[EARLY_COUNT * pairs] if early else pairs - plan[EARLY_COUNT * pairs]
    first = 0 if early else plan[EARLY_COUNT * pairs]
    pair = lambda s: plan[EARLY * pairs + first + s]

    def fetch(s, slot):
        right = plan[RIGHT * pairs + pair(s)]
        for base, pieces in sources:
            for o in range(orbitals):

                @pl.when(right == base + o)
                def _():
                    at = 0
                    for piece in pieces:
                        target = right_buf.at[slot, pl.ds(at, piece.shape[1])]
                        pltpu.make_async_copy(piece.at[o], target, right_sem.at[slot]).start()
                        at += piece.shape[1]

    def arrived(slot):
        pltpu.make_async_copy(slabs.at[0], right_buf.at[slot], right_sem.at[slot]).wait()

    def store(s, slot):
        return pltpu.make_async_copy(out_buf.at[slot], out.at[pair(s)], out_sem.at[slot])

    lefts = [pltpu.make_async_copy(slabs.at[o], left_buf.at[o], left_sem.at[o]) for o in range(orbitals)]
    for copy in lefts:
        copy.start()

    @pl.when(count > 0)
    def _():
        fetch(0, 0)

    for o in range(orbitals):
        lefts[o].wait()
        high[o], low[o] = split(left_buf[o])

    def one(s, carry):
        slot = s % 2

        @pl.when(s + 1 < count)
        def _():
            fetch(s + 1, 1 - slot)

        arrived(slot)

        @pl.when(s >= 2)
        def _():
            store(s - 2, slot).wait()

        left = plan[LEFT * pairs + pair(s)]
        rh, rl = split(right_buf[slot])
        wide = dot_nt(high[left], jnp.concatenate([rh, rl], axis=0))
        out_buf[slot] = wide[:, :nv] + wide[:, nv:] + dot_nt(low[left], rh)
        store(s, slot).start()
        return carry

    lax.fori_loop(0, count, one, 0)

    @pl.when(count >= 2)
    def _():
        store(count - 2, count % 2).wait()

    @pl.when(count >= 1)
    def _():
        store(count - 1, (count + 1) % 2).wait()


def pair_integrals(early, plan, slabs, pairs, groups, done=None):
    orbitals, nv, nq = slabs.shape
    operands = [plan, slabs]
    for group in groups:
        operands += group
    in_specs = [SMEM] + [ANY] * (len(operands) - 1)
    aliases = {}
    if done is not None:
        aliases = {len(operands): 0}
        operands.append(done)
        in_specs.append(ANY)
    return pl.pallas_call(
        functools.partial(integrals_kernel, early, [len(group) for group in groups]),
        out_shape=jax.ShapeDtypeStruct((pairs, nv, nv), f32),
        in_specs=in_specs,
        out_specs=ANY,
        scratch_shapes=[
            pltpu.VMEM((orbitals, nv, nq), f32),
            pltpu.VMEM((orbitals, nv, nq), bf16),
            pltpu.VMEM((orbitals, nv, nq), bf16),
            pltpu.VMEM((2, nv, nq), f32),
            pltpu.VMEM((2, nv, nv), f32),
            pltpu.SemaphoreType.DMA((orbitals,)),
            pltpu.SemaphoreType.DMA((2,)),
            pltpu.SemaphoreType.DMA((2,)),
        ],
        input_output_aliases=aliases,
        compiler_params=PARAMS,
        cost_estimate=cost(pairs * 3 * nv * nv * nq, pairs * 2 * nv * nq),
        name="pair_integrals",
    )(*operands)


def shards(slabs, amplitudes, intersections, fock_coupling, virt_energy, occ_pair_energy, pair_orbs, couplings):
    axis = "orb"
    count = lax.axis_size(axis)
    device = lax.axis_index(axis)
    selects_near = device % 2 == (device // 2) % 2
    orbitals, nv, nq = slabs.shape
    pairs = amplitudes.shape[0]
    half = pairs // 2

    everyone = range(count)
    chip_odd = lambda i: (i // 2) % 2
    inside = [(i, i ^ 1) for i in everyone]
    beside = [(i, (i + 1) % count if i % 2 else (i - 1) % count) for i in everyone]
    near_perm = [(i, i ^ 2) for i in everyone]
    far_perm = [(i, (i - 4 if chip_odd(i) else i + 4) % count) for i in everyone]
    send = lambda value, perm: lax.ppermute(value, axis, perm)

    lists_cross = send(couplings, beside)
    rows = nv // CHUNKS
    pieces = [slabs[:, k * rows : (k + 1) * rows] for k in range(CHUNKS)]
    *pieces, lists_cross = lax.optimization_barrier((*pieces, lists_cross))
    near = [send(piece, near_perm) for piece in pieces]
    intra_t = send(amplitudes, inside)
    slabs_swapped = send(slabs, inside)

    core = device % 2
    partner = device + 1 - 2 * core
    intra_list = jnp.where(core == 0, couplings[:, 1], couplings[:, 0])
    coupled_rows = jnp.concatenate(
        [couplings[:, 2] - device * pairs, intra_list - partner * pairs, jnp.stack([2 + 0 * core, 1 - core])]
    )

    partial = couple(0, 0, pairs, after(coupled_rows, *pieces), intersections, amplitudes, fock_coupling)
    near[0], partial = lax.optimization_barrier((near[0], partial))
    far = [send(near[0], far_perm)]
    partial = couple(1, 0, pairs, coupled_rows, intersections, intra_t, fock_coupling, partial, True)
    near[1], partial = lax.optimization_barrier((near[1], partial))
    far.append(send(near[1], far_perm))

    where = after(device.astype(jnp.int32).reshape(1), near[1])
    plan = make_plan(count, orbitals, where, couplings, lists_cross, pair_orbs)
    across, down = virt_energy, virt_energy.T
    cross_out = gather_rows(plan, amplitudes)
    cross_t = [send(rows_out, beside) for rows_out in cross_out]
    near[2], far[0], plan, *_ = lax.optimization_barrier((near[2], far[0], plan, *cross_out))
    far.append(send(near[2], far_perm))
    integrals = pair_integrals(True, plan, slabs, pairs, [[slabs_swapped], near])
    far[2], integrals = lax.optimization_barrier((far[2], integrals))
    relayed = [send(jnp.where(selects_near, n, f), inside) for n, f in zip(near, far)]
    integrals = pair_integrals(False, plan, slabs, pairs, [far, relayed], integrals)

    current = amplitudes
    for iteration in range(ITERS):
        if iteration > 0:
            cross_t = [send(rows_out, beside) for rows_out in cross_out]
            intra_t = send(current, inside)
            partial = couple(0, 0, pairs, coupled_rows, intersections, current, fock_coupling)
            partial = couple(1, 0, pairs, coupled_rows, intersections, intra_t, fock_coupling, partial, True)
        sending = iteration + 1 < ITERS
        done = None
        for k, (low, high) in enumerate(rank_groups(half, iteration)):
            done = finish(
                low,
                high,
                sending,
                plan,
                intersections,
                cross_t[k],
                fock_coupling,
                partial,
                integrals,
                current,
                across,
                down,
                occ_pair_energy,
                done,
            )
        current = done[0]
        if sending:
            cross_out = done[1:]
    return current


def solution(mesh):
    in_specs = (
        P("orb", None, None),
        P("orb", None, None),
        P("orb", None, None, None),
        P("orb", None),
        P("orb", None),
        P("orb"),
        P("orb", None),
        P("orb", None),
    )
    out_specs = P("orb", None, None)
    return jax.shard_map(shards, mesh=mesh, in_specs=in_specs, out_specs=out_specs, check_vma=False)
```

```python
import functools

import jax
import jax.numpy as jnp
from jax import lax
from jax.experimental import pallas as pl
from jax.experimental.pallas import tpu as pltpu
from jax.sharding import PartitionSpec as P

REACH = 2
ITERS = 2
CHUNKS = 3

f32 = jnp.float32
bf16 = jnp.bfloat16
ANY = pl.BlockSpec(memory_space=pl.ANY)
SMEM = pl.BlockSpec(memory_space=pltpu.SMEM)
VMEM = pl.BlockSpec(memory_space=pltpu.VMEM)
PARAMS = pltpu.CompilerParams(vmem_limit_bytes=127 * 512 * 1024)

CROSS, ORDER, START, SEND, EARLY, EARLY_COUNT, LEFT, RIGHT, COLUMN, SECTIONS = range(10)


def after(value, *earlier):
    return lax.optimization_barrier((value,) + earlier)[0]


def cost(flops, moved):
    return pl.CostEstimate(flops=flops // 1000, bytes_accessed=moved // 1000, transcendentals=0)


def split(x):
    hi = x.astype(bf16)
    lo = (x - hi.astype(f32)).astype(bf16)
    return hi, lo


def dot_nn(a, b):
    return lax.dot_general(a, b, (((1,), (0,)), ((), ())), preferred_element_type=f32)


def dot_nt(a, b):
    return lax.dot_general(a, b, (((1,), (1,)), ((), ())), preferred_element_type=f32)


def project(x, t, gain):
    nv = x.shape[0]
    xh, xl = split(x)
    th, tl = split(t)
    wide = dot_nn(xh, jnp.concatenate([th, tl], axis=1))
    half = wide[:, :nv] + wide[:, nv:] + dot_nn(xl, th)
    hh, hl = split(half * gain)
    wide = dot_nt(hh, jnp.concatenate([xh, xl], axis=0))
    return wide[:, :nv] + wide[:, nv:] + dot_nt(hl, xh)


def plan_kernel(devices, orbitals, where, couplings, lists_cross, pair_orbs, plan, seen):
    pairs = couplings.shape[0]
    half = pairs // 2
    device = where[0]
    core = device % 2
    odd = (device // 2) % 2
    outside = (device - 1 + 2 * core + devices) % devices

    def mark(lists, column, base):
        for q in range(pairs):
            seen[q] = 0
        for p in range(pairs):
            seen[lists[p, column] - base] = 1

    def ranks(lists, column, base, section):
        mark(lists, column, base)
        below = jnp.int32(0)
        for q in range(pairs):
            here = seen[q]
            seen[q] = below
            below = below + here
        for p in range(pairs):
            plan[section * pairs + p] = jnp.minimum(seen[lists[p, column] - base], half - 1)

    def sends(lists, column, section):
        mark(lists, column, device * pairs)
        below = jnp.int32(0)
        for q in range(pairs):
            here = seen[q]
            plan[section * pairs + q] = jnp.where(jnp.logical_and(here == 1, below < half), below, -1)
            below = below + here

    def sort(section, key, keys, cuts):
        filled = jnp.int32(0)
        for k in range(keys):
            if cuts is not None:
                plan[cuts * pairs + k] = filled
            for p in range(pairs):
                mine = key(p) == k

                @pl.when(mine)
                def _():
                    plan[section * pairs + filled] = p

                filled = filled + mine.astype(jnp.int32)
        if cuts is not None:
            plan[cuts * pairs + keys] = filled

    ranks(couplings, core, outside * pairs, CROSS)
    sends(lists_cross, 1 - core, SEND)
    sort(ORDER, lambda p: plan[CROSS * pairs + p], half, START)

    swapped = (REACH + 1 - 2 * core) * orbitals
    near = (1 - odd) * 2 * REACH * orbitals
    late = jnp.int32(0)
    for p in range(pairs):
        right = pair_orbs[p, 1] - (device - REACH) * orbitals
        plan[LEFT * pairs + p] = pair_orbs[p, 0] - device * orbitals
        plan[RIGHT * pairs + p] = right
        first = jnp.logical_or(
            jnp.logical_and(right >= swapped, right < swapped + orbitals),
            jnp.logical_and(right >= near, right < near + orbitals),
        )
        seen[p] = 1 - first.astype(jnp.int32)
        late = late + seen[p]
    sort(EARLY, lambda p: seen[p], 2, None)
    plan[EARLY_COUNT * pairs] = pairs - late
    plan[COLUMN * pairs + 1] = core
    plan[COLUMN * pairs + 2] = swapped
    plan[COLUMN * pairs + 3] = near
    plan[COLUMN * pairs + 4] = 2 * REACH * orbitals - near
    plan[COLUMN * pairs + 5] = 2 * REACH * orbitals - swapped


def make_plan(devices, orbitals, where, couplings, lists_cross, pair_orbs):
    pairs = couplings.shape[0]
    return pl.pallas_call(
        functools.partial(plan_kernel, devices, orbitals),
        out_shape=jax.ShapeDtypeStruct((SECTIONS * pairs,), jnp.int32),
        in_specs=[SMEM] * 4,
        out_specs=SMEM,
        scratch_shapes=[pltpu.SMEM((pairs,), jnp.int32)],
        name="plan",
    )(where, couplings, lists_cross, pair_orbs)


def send_copies(p, plan, source, outs, sem, act):
    pairs = plan.shape[0] // SECTIONS
    place = plan[SEND * pairs + p]
    rank = 0
    for out in outs:
        for r in range(out.shape[0]):

            @pl.when(place == rank)
            def _():
                act(pltpu.make_async_copy(source, out.at[r], sem.at[place]))

            rank += 1


def start(copy):
    copy.start()


def wait(copy):
    copy.wait()


def rank_groups(half, iteration):
    cut = half // 2 if iteration == 0 else half - 1
    return [(0, cut), (cut, half)]


def send_shapes(half, nv, iteration):
    return [jax.ShapeDtypeStruct((high - low, nv, nv), f32) for low, high in rank_groups(half, iteration)]


def gather_kernel(plan, current, *rest):
    outs, (rows, load_sem, send_sem) = rest[:-3], rest[-3:]
    pairs = current.shape[0]
    loads = [pltpu.make_async_copy(current.at[p], rows.at[p], load_sem.at[p]) for p in range(pairs)]

    def chosen(p, act):
        @pl.when(plan[SEND * pairs + p] >= 0)
        def _():
            act(loads[p])

    for p in range(pairs):
        chosen(p, start)
    for p in range(pairs):
        chosen(p, wait)
        send_copies(p, plan, rows.at[p], outs, send_sem, start)
    for p in range(pairs):
        send_copies(p, plan, rows.at[p], outs, send_sem, wait)


def gather_rows(plan, current):
    pairs, nv, _ = current.shape
    half = pairs // 2
    shapes = send_shapes(half, nv, 0)
    return pl.pallas_call(
        gather_kernel,
        out_shape=shapes,
        in_specs=[SMEM, ANY],
        out_specs=[ANY] * len(shapes),
        scratch_shapes=[
            pltpu.VMEM((pairs, nv, nv), f32),
            pltpu.SemaphoreType.DMA((pairs,)),
            pltpu.SemaphoreType.DMA((half,)),
        ],
        compiler_params=PARAMS,
        cost_estimate=cost(0, 2 * half * nv * nv * 4),
        name="gather_rows",
    )(plan, current)


def couple_kernel(kind, low, pairs, adding, rows, x, t, gain, *rest):
    p = low + pl.program_id(0)
    value = project(x[0, 0], t[0], gain[p, rows[2 * pairs + kind]])
    rest[-1][0] = rest[0][0] + value if adding else value


def couple(kind, low, high, rows, x, t, gain, before=None, adding=False):
    pairs, _, nv, _ = x.shape
    square = pl.BlockSpec((1, nv, nv), lambda p, rows: (low + p, 0, 0))
    in_specs = [
        pl.BlockSpec((1, 1, nv, nv), lambda p, rows: (low + p, rows[2 * pairs + kind], 0, 0)),
        pl.BlockSpec((1, nv, nv), lambda p, rows: (rows[kind * pairs + low + p], 0, 0)),
        SMEM,
    ]
    operands = [x, t, gain]
    if before is not None:
        in_specs.append(square if adding else ANY)
        operands.append(before)
    return pl.pallas_call(
        functools.partial(couple_kernel, kind, low, pairs, adding),
        out_shape=jax.ShapeDtypeStruct((pairs, nv, nv), f32),
        grid_spec=pltpu.PrefetchScalarGridSpec(
            num_scalar_prefetch=1, grid=(high - low,), in_specs=in_specs, out_specs=square
        ),
        input_output_aliases={} if before is None else {4: 0},
        compiler_params=PARAMS,
        cost_estimate=cost((high - low) * 12 * nv**3, (high - low) * nv * nv * 12),
        name="couple",
    )(rows, *operands)


def finish_kernel(low, high, sending, plan, gain, occ, across, down, x, before, integral, own, *rest):
    rest, scratch = rest[:-10], rest[-10:]
    x_buf, t_buf, before_buf, integral_buf, own_buf, out_buf, sem, t_sem, out_sem, send_sem = scratch
    pairs = x.shape[0]
    t = rest[0]
    outs = rest[len(rest) - (3 if sending else 1) :]
    out = outs[0]
    first = plan[START * pairs + low]
    count = plan[START * pairs + high] - first
    column = plan[COLUMN * pairs + 1]
    pair = lambda s: plan[ORDER * pairs + first + s]

    def fetch(s, slot):
        p = pair(s)
        return (
            pltpu.make_async_copy(x.at[p, column], x_buf.at[slot], sem.at[slot, 0]),
            pltpu.make_async_copy(before.at[p], before_buf.at[slot], sem.at[slot, 1]),
            pltpu.make_async_copy(integral.at[p], integral_buf.at[slot], sem.at[slot, 2]),
            pltpu.make_async_copy(own.at[p], own_buf.at[slot], sem.at[slot, 3]),
        )

    def stores(s, act):
        p = pair(s)
        act(pltpu.make_async_copy(out_buf.at[s], out.at[p], out_sem.at[s]))
        if sending:
            send_copies(p, plan, out_buf.at[s], outs[1:], send_sem, act)

    t_copies = [pltpu.make_async_copy(t.at[k], t_buf.at[k], t_sem.at[k]) for k in range(high - low)]

    for copy in t_copies:
        copy.start()

    @pl.when(count > 0)
    def _():
        for copy in fetch(0, 0):
            copy.start()

    for copy in t_copies:
        copy.wait()

    def one(s, carry):
        slot = s % 2

        @pl.when(s + 1 < count)
        def _():
            for copy in fetch(s + 1, 1 - slot):
                copy.start()

        x_copy, *other_copies = fetch(s, slot)
        x_copy.wait()
        p = pair(s)
        picked = t_buf[plan[CROSS * pairs + p] - low]
        coupled = project(x_buf[slot], picked, gain[p, column])
        for copy in other_copies:
            copy.wait()
        coupled = before_buf[slot] + coupled
        lane = lax.broadcasted_iota(jnp.int32, down.shape, 1)
        tall = jnp.sum(jnp.where(lane == p, down[...], 0.0), axis=1, keepdims=True)
        denominator = tall + across[pl.ds(p, 1), :] - occ[p]
        mine = own_buf[slot]
        residual = integral_buf[slot] + denominator * mine - coupled
        out_buf[s] = mine - residual / denominator
        stores(s, start)
        return carry

    lax.fori_loop(0, count, one, 0)

    def end(s, carry):
        stores(s, wait)
        return carry

    lax.fori_loop(0, count, end, 0)


def finish(low, high, sending, plan, x, t, gain, before, integral, own, across, down, occ, done):
    pairs, _, nv, _ = x.shape
    half = pairs // 2
    operands = [plan, gain, occ, across, down, x, before, integral, own, t]
    in_specs = [SMEM] * 3 + [VMEM] * 2 + [ANY] * 5
    out_shape = [jax.ShapeDtypeStruct((pairs, nv, nv), f32)]
    if sending:
        out_shape += send_shapes(half, nv, 1)
    aliases = {}
    if done is not None:
        aliases = {len(operands) + k: k for k in range(len(done))}
        in_specs += [ANY] * len(done)
        operands += done
    two = pltpu.VMEM((2, nv, nv), f32)
    return pl.pallas_call(
        functools.partial(finish_kernel, low, high, sending),
        out_shape=out_shape,
        in_specs=in_specs,
        out_specs=[ANY] * len(out_shape),
        scratch_shapes=[
            two,
            pltpu.VMEM((high - low, nv, nv), f32),
            two,
            two,
            two,
            pltpu.VMEM((pairs, nv, nv), f32),
            pltpu.SemaphoreType.DMA((2, 4)),
            pltpu.SemaphoreType.DMA((high - low,)),
            pltpu.SemaphoreType.DMA((pairs,)),
            pltpu.SemaphoreType.DMA((half,)),
        ],
        input_output_aliases=aliases,
        compiler_params=PARAMS,
        cost_estimate=cost(2 * (high - low) * 12 * nv**3, 2 * (high - low) * nv * nv * 24),
        name="finish",
    )(*operands)


def integrals_kernel(early, groups, plan, slabs, *rest):
    rest, (left_buf, high, low, right_buf, out_buf, left_sem, right_sem, out_sem) = rest[:-8], rest[-8:]
    out = rest[-1]
    orbitals, nv, nq = slabs.shape
    pairs = out.shape[0]
    sources, used = [], 0
    for k, pieces in enumerate(groups):
        sources.append((plan[COLUMN * pairs + (2 if early else 4) + k], rest[used : used + pieces]))
        used += pieces
    count = plan[EARLY_COUNT * pairs] if early else pairs - plan[EARLY_COUNT * pairs]
    first = 0 if early else plan[EARLY_COUNT * pairs]
    pair = lambda s: plan[EARLY * pairs + first + s]

    def fetch(s, slot):
        right = plan[RIGHT * pairs + pair(s)]
        for base, pieces in sources:
            for o in range(orbitals):

                @pl.when(right == base + o)
                def _():
                    at = 0
                    for piece in pieces:
                        target = right_buf.at[slot, pl.ds(at, piece.shape[1])]
                        pltpu.make_async_copy(piece.at[o], target, right_sem.at[slot]).start()
                        at += piece.shape[1]

    def arrived(slot):
        pltpu.make_async_copy(slabs.at[0], right_buf.at[slot], right_sem.at[slot]).wait()

    def store(s, slot):
        return pltpu.make_async_copy(out_buf.at[slot], out.at[pair(s)], out_sem.at[slot])

    lefts = [pltpu.make_async_copy(slabs.at[o], left_buf.at[o], left_sem.at[o]) for o in range(orbitals)]
    for copy in lefts:
        copy.start()

    @pl.when(count > 0)
    def _():
        fetch(0, 0)

    for o in range(orbitals):
        lefts[o].wait()
        high[o], low[o] = split(left_buf[o])

    def one(s, carry):
        slot = s % 2

        @pl.when(s + 1 < count)
        def _():
            fetch(s + 1, 1 - slot)

        arrived(slot)

        @pl.when(s >= 2)
        def _():
            store(s - 2, slot).wait()

        left = plan[LEFT * pairs + pair(s)]
        rh, rl = split(right_buf[slot])
        wide = dot_nt(high[left], jnp.concatenate([rh, rl], axis=0))
        out_buf[slot] = wide[:, :nv] + wide[:, nv:] + dot_nt(low[left], rh)
        store(s, slot).start()
        return carry

    lax.fori_loop(0, count, one, 0)

    @pl.when(count >= 2)
    def _():
        store(count - 2, count % 2).wait()

    @pl.when(count >= 1)
    def _():
        store(count - 1, (count + 1) % 2).wait()


def pair_integrals(early, plan, slabs, pairs, groups, done=None):
    orbitals, nv, nq = slabs.shape
    operands = [plan, slabs]
    for group in groups:
        operands += group
    in_specs = [SMEM] + [ANY] * (len(operands) - 1)
    aliases = {}
    if done is not None:
        aliases = {len(operands): 0}
        operands.append(done)
        in_specs.append(ANY)
    return pl.pallas_call(
        functools.partial(integrals_kernel, early, [len(group) for group in groups]),
        out_shape=jax.ShapeDtypeStruct((pairs, nv, nv), f32),
        in_specs=in_specs,
        out_specs=ANY,
        scratch_shapes=[
            pltpu.VMEM((orbitals, nv, nq), f32),
            pltpu.VMEM((orbitals, nv, nq), bf16),
            pltpu.VMEM((orbitals, nv, nq), bf16),
            pltpu.VMEM((2, nv, nq), f32),
            pltpu.VMEM((2, nv, nv), f32),
            pltpu.SemaphoreType.DMA((orbitals,)),
            pltpu.SemaphoreType.DMA((2,)),
            pltpu.SemaphoreType.DMA((2,)),
        ],
        input_output_aliases=aliases,
        compiler_params=PARAMS,
        cost_estimate=cost(pairs * 3 * nv * nv * nq, pairs * 2 * nv * nq),
        name="pair_integrals",
    )(*operands)


def shards(slabs, amplitudes, intersections, fock_coupling, virt_energy, occ_pair_energy, pair_orbs, couplings):
    axis = "orb"
    count = lax.axis_size(axis)
    device = lax.axis_index(axis)
    selects_near = device % 2 == (device // 2) % 2
    orbitals, nv, nq = slabs.shape
    pairs = amplitudes.shape[0]
    half = pairs // 2

    everyone = range(count)
    chip_odd = lambda i: (i // 2) % 2
    inside = [(i, i ^ 1) for i in everyone]
    beside = [(i, (i + 1) % count if i % 2 else (i - 1) % count) for i in everyone]
    near_perm = [(i, i ^ 2) for i in everyone]
    far_perm = [(i, (i - 4 if chip_odd(i) else i + 4) % count) for i in everyone]
    send = lambda value, perm: lax.ppermute(value, axis, perm)

    lists_cross = send(couplings, beside)
    rows = nv // CHUNKS
    pieces = [slabs[:, k * rows : (k + 1) * rows] for k in range(CHUNKS)]
    *pieces, lists_cross = lax.optimization_barrier((*pieces, lists_cross))
    near = [send(piece, near_perm) for piece in pieces]
    intra_t = send(amplitudes, inside)
    slabs_swapped = send(slabs, inside)

    core = device % 2
    partner = device + 1 - 2 * core
    intra_list = jnp.where(core == 0, couplings[:, 1], couplings[:, 0])
    coupled_rows = jnp.concatenate(
        [couplings[:, 2] - device * pairs, intra_list - partner * pairs, jnp.stack([2 + 0 * core, 1 - core])]
    )

    partial = couple(0, 0, pairs, after(coupled_rows, *pieces), intersections, amplitudes, fock_coupling)
    near[0], partial = lax.optimization_barrier((near[0], partial))
    far = [send(near[0], far_perm)]
    partial = couple(1, 0, pairs, coupled_rows, intersections, intra_t, fock_coupling, partial, True)
    near[1], partial = lax.optimization_barrier((near[1], partial))
    far.append(send(near[1], far_perm))

    where = after(device.astype(jnp.int32).reshape(1), near[1])
    plan = make_plan(count, orbitals, where, couplings, lists_cross, pair_orbs)
    across, down = virt_energy, virt_energy.T
    cross_out = gather_rows(plan, amplitudes)
    cross_t = [send(rows_out, beside) for rows_out in cross_out]
    near[2], far[0], plan, *_ = lax.optimization_barrier((near[2], far[0], plan, *cross_out))
    far.append(send(near[2], far_perm))
    integrals = pair_integrals(True, plan, slabs, pairs, [[slabs_swapped], near])
    far[2], integrals = lax.optimization_barrier((far[2], integrals))
    relayed = [send(jnp.where(selects_near, n, f), inside) for n, f in zip(near, far)]
    integrals = pair_integrals(False, plan, slabs, pairs, [far, relayed], integrals)

    current = amplitudes
    for iteration in range(ITERS):
        if iteration > 0:
            cross_t = [send(rows_out, beside) for rows_out in cross_out]
            intra_t = send(current, inside)
            partial = couple(0, 0, pairs, coupled_rows, intersections, current, fock_coupling)
            partial = couple(1, 0, pairs, coupled_rows, intersections, intra_t, fock_coupling, partial, True)
        sending = iteration + 1 < ITERS
        done = None
        for k, (low, high) in enumerate(rank_groups(half, iteration)):
            done = finish(
                low,
                high,
                sending,
                plan,
                intersections,
                cross_t[k],
                fock_coupling,
                partial,
                integrals,
                current,
                across,
                down,
                occ_pair_energy,
                done,
            )
        current = done[0]
        if sending:
            cross_out = done[1:]
    return current


def solution(mesh):
    in_specs = (
        P("orb", None, None),
        P("orb", None, None),
        P("orb", None, None, None),
        P("orb", None),
        P("orb", None),
        P("orb"),
        P("orb", None),
        P("orb", None),
    )
    out_specs = P("orb", None, None)
    return jax.shard_map(shards, mesh=mesh, in_specs=in_specs, out_specs=out_specs, check_vma=False)
```

```python
import functools

import jax
import jax.numpy as jnp
from jax import lax
from jax.experimental import pallas as pl
from jax.experimental.pallas import tpu as pltpu
from jax.sharding import PartitionSpec as P

REACH = 2
ITERS = 2
CHUNKS = 3

f32 = jnp.float32
bf16 = jnp.bfloat16
ANY = pl.BlockSpec(memory_space=pl.ANY)
SMEM = pl.BlockSpec(memory_space=pltpu.SMEM)
VMEM = pl.BlockSpec(memory_space=pltpu.VMEM)
PARAMS = pltpu.CompilerParams(vmem_limit_bytes=127 * 512 * 1024)

CROSS, ORDER, START, SEND, EARLY, EARLY_COUNT, LEFT, RIGHT, COLUMN, SECTIONS = range(10)


def after(value, *earlier):
    return lax.optimization_barrier((value,) + earlier)[0]


def cost(flops, moved):
    return pl.CostEstimate(flops=flops // 1000, bytes_accessed=moved // 1000, transcendentals=0)


def split(x):
    hi = x.astype(bf16)
    lo = (x - hi.astype(f32)).astype(bf16)
    return hi, lo


def dot_nn(a, b):
    return lax.dot_general(a, b, (((1,), (0,)), ((), ())), preferred_element_type=f32)


def dot_nt(a, b):
    return lax.dot_general(a, b, (((1,), (1,)), ((), ())), preferred_element_type=f32)


def project(x, t, gain):
    nv = x.shape[0]
    xh, xl = split(x)
    th, tl = split(t)
    wide = dot_nn(xh, jnp.concatenate([th, tl], axis=1))
    half = wide[:, :nv] + wide[:, nv:] + dot_nn(xl, th)
    hh, hl = split(half * gain)
    wide = dot_nt(hh, jnp.concatenate([xh, xl], axis=0))
    return wide[:, :nv] + wide[:, nv:] + dot_nt(hl, xh)


def plan_kernel(devices, orbitals, where, couplings, lists_cross, pair_orbs, plan, seen):
    pairs = couplings.shape[0]
    half = pairs // 2
    device = where[0]
    core = device % 2
    odd = (device // 2) % 2
    outside = (device - 1 + 2 * core + devices) % devices

    def mark(lists, column, base):
        for q in range(pairs):
            seen[q] = 0
        for p in range(pairs):
            seen[lists[p, column] - base] = 1

    def ranks(lists, column, base, section):
        mark(lists, column, base)
        below = jnp.int32(0)
        for q in range(pairs):
            here = seen[q]
            seen[q] = below
            below = below + here
        for p in range(pairs):
            plan[section * pairs + p] = jnp.minimum(seen[lists[p, column] - base], half - 1)

    def sends(lists, column, section):
        mark(lists, column, device * pairs)
        below = jnp.int32(0)
        for q in range(pairs):
            here = seen[q]
            plan[section * pairs + q] = jnp.where(jnp.logical_and(here == 1, below < half), below, -1)
            below = below + here

    def sort(section, key, keys, cuts):
        filled = jnp.int32(0)
        for k in range(keys):
            if cuts is not None:
                plan[cuts * pairs + k] = filled
            for p in range(pairs):
                mine = key(p) == k

                @pl.when(mine)
                def _():
                    plan[section * pairs + filled] = p

                filled = filled + mine.astype(jnp.int32)
        if cuts is not None:
            plan[cuts * pairs + keys] = filled

    ranks(couplings, core, outside * pairs, CROSS)
    sends(lists_cross, 1 - core, SEND)
    sort(ORDER, lambda p: plan[CROSS * pairs + p], half, START)

    swapped = (REACH + 1 - 2 * core) * orbitals
    near = (1 - odd) * 2 * REACH * orbitals
    late = jnp.int32(0)
    for p in range(pairs):
        right = pair_orbs[p, 1] - (device - REACH) * orbitals
        plan[LEFT * pairs + p] = pair_orbs[p, 0] - device * orbitals
        plan[RIGHT * pairs + p] = right
        first = jnp.logical_or(
            jnp.logical_and(right >= swapped, right < swapped + orbitals),
            jnp.logical_and(right >= near, right < near + orbitals),
        )
        seen[p] = 1 - first.astype(jnp.int32)
        late = late + seen[p]
    sort(EARLY, lambda p: seen[p], 2, None)
    plan[EARLY_COUNT * pairs] = pairs - late
    plan[COLUMN * pairs + 1] = core
    plan[COLUMN * pairs + 2] = swapped
    plan[COLUMN * pairs + 3] = near
    plan[COLUMN * pairs + 4] = 2 * REACH * orbitals - near
    plan[COLUMN * pairs + 5] = 2 * REACH * orbitals - swapped


def make_plan(devices, orbitals, where, couplings, lists_cross, pair_orbs):
    pairs = couplings.shape[0]
    return pl.pallas_call(
        functools.partial(plan_kernel, devices, orbitals),
        out_shape=jax.ShapeDtypeStruct((SECTIONS * pairs,), jnp.int32),
        in_specs=[SMEM] * 4,
        out_specs=SMEM,
        scratch_shapes=[pltpu.SMEM((pairs,), jnp.int32)],
        name="plan",
    )(where, couplings, lists_cross, pair_orbs)


def send_copies(p, plan, source, outs, sem, act):
    pairs = plan.shape[0] // SECTIONS
    place = plan[SEND * pairs + p]
    rank = 0
    for out in outs:
        for r in range(out.shape[0]):

            @pl.when(place == rank)
            def _():
                act(pltpu.make_async_copy(source, out.at[r], sem.at[place]))

            rank += 1


def start(copy):
    copy.start()


def wait(copy):
    copy.wait()


def rank_groups(half, iteration):
    cut = half // 2 if iteration == 0 else half - 1
    return [(0, cut), (cut, half)]


def send_shapes(half, nv, iteration):
    return [jax.ShapeDtypeStruct((high - low, nv, nv), f32) for low, high in rank_groups(half, iteration)]


def gather_kernel(plan, current, *rest):
    outs, (rows, load_sem, send_sem) = rest[:-3], rest[-3:]
    pairs = current.shape[0]
    loads = [pltpu.make_async_copy(current.at[p], rows.at[p], load_sem.at[p]) for p in range(pairs)]

    def chosen(p, act):
        @pl.when(plan[SEND * pairs + p] >= 0)
        def _():
            act(loads[p])

    for p in range(pairs):
        chosen(p, start)
    for p in range(pairs):
        chosen(p, wait)
        send_copies(p, plan, rows.at[p], outs, send_sem, start)
    for p in range(pairs):
        send_copies(p, plan, rows.at[p], outs, send_sem, wait)


def gather_rows(plan, current):
    pairs, nv, _ = current.shape
    half = pairs // 2
    shapes = send_shapes(half, nv, 0)
    return pl.pallas_call(
        gather_kernel,
        out_shape=shapes,
        in_specs=[SMEM, ANY],
        out_specs=[ANY] * len(shapes),
        scratch_shapes=[
            pltpu.VMEM((pairs, nv, nv), f32),
            pltpu.SemaphoreType.DMA((pairs,)),
            pltpu.SemaphoreType.DMA((half,)),
        ],
        compiler_params=PARAMS,
        cost_estimate=cost(0, 2 * half * nv * nv * 4),
        name="gather_rows",
    )(plan, current)


def couple_kernel(kind, low, pairs, adding, rows, x, t, gain, *rest):
    p = low + pl.program_id(0)
    value = project(x[0, 0], t[0], gain[p, rows[2 * pairs + kind]])
    rest[-1][0] = rest[0][0] + value if adding else value


def couple(kind, low, high, rows, x, t, gain, before=None, adding=False):
    pairs, _, nv, _ = x.shape
    square = pl.BlockSpec((1, nv, nv), lambda p, rows: (low + p, 0, 0))
    in_specs = [
        pl.BlockSpec((1, 1, nv, nv), lambda p, rows: (low + p, rows[2 * pairs + kind], 0, 0)),
        pl.BlockSpec((1, nv, nv), lambda p, rows: (rows[kind * pairs + low + p], 0, 0)),
        SMEM,
    ]
    operands = [x, t, gain]
    if before is not None:
        in_specs.append(square if adding else ANY)
        operands.append(before)
    return pl.pallas_call(
        functools.partial(couple_kernel, kind, low, pairs, adding),
        out_shape=jax.ShapeDtypeStruct((pairs, nv, nv), f32),
        grid_spec=pltpu.PrefetchScalarGridSpec(
            num_scalar_prefetch=1, grid=(high - low,), in_specs=in_specs, out_specs=square
        ),
        input_output_aliases={} if before is None else {4: 0},
        compiler_params=PARAMS,
        cost_estimate=cost((high - low) * 12 * nv**3, (high - low) * nv * nv * 12),
        name="couple",
    )(rows, *operands)


def finish_kernel(low, high, sending, plan, gain, occ, across, down, x, before, integral, own, *rest):
    rest, scratch = rest[:-10], rest[-10:]
    x_buf, t_buf, before_buf, integral_buf, own_buf, out_buf, sem, t_sem, out_sem, send_sem = scratch
    pairs = x.shape[0]
    t = rest[0]
    outs = rest[len(rest) - (3 if sending else 1) :]
    out = outs[0]
    first = plan[START * pairs + low]
    count = plan[START * pairs + high] - first
    column = plan[COLUMN * pairs + 1]
    pair = lambda s: plan[ORDER * pairs + first + s]

    def fetch(s, slot):
        p = pair(s)
        return (
            pltpu.make_async_copy(x.at[p, column], x_buf.at[slot], sem.at[slot, 0]),
            pltpu.make_async_copy(before.at[p], before_buf.at[slot], sem.at[slot, 1]),
            pltpu.make_async_copy(integral.at[p], integral_buf.at[slot], sem.at[slot, 2]),
            pltpu.make_async_copy(own.at[p], own_buf.at[slot], sem.at[slot, 3]),
        )

    def stores(s, act):
        p = pair(s)
        act(pltpu.make_async_copy(out_buf.at[s], out.at[p], out_sem.at[s]))
        if sending:
            send_copies(p, plan, out_buf.at[s], outs[1:], send_sem, act)

    t_copies = [pltpu.make_async_copy(t.at[k], t_buf.at[k], t_sem.at[k]) for k in range(high - low)]

    for copy in t_copies:
        copy.start()

    @pl.when(count > 0)
    def _():
        for copy in fetch(0, 0):
            copy.start()

    for copy in t_copies:
        copy.wait()

    def one(s, carry):
        slot = s % 2

        @pl.when(s + 1 < count)
        def _():
            for copy in fetch(s + 1, 1 - slot):
                copy.start()

        x_copy, *other_copies = fetch(s, slot)
        x_copy.wait()
        p = pair(s)
        picked = t_buf[plan[CROSS * pairs + p] - low]
        coupled = project(x_buf[slot], picked, gain[p, column])
        for copy in other_copies:
            copy.wait()
        coupled = before_buf[slot] + coupled
        lane = lax.broadcasted_iota(jnp.int32, down.shape, 1)
        tall = jnp.sum(jnp.where(lane == p, down[...], 0.0), axis=1, keepdims=True)
        denominator = tall + across[pl.ds(p, 1), :] - occ[p]
        mine = own_buf[slot]
        residual = integral_buf[slot] + denominator * mine - coupled
        out_buf[s] = mine - residual / denominator
        stores(s, start)
        return carry

    lax.fori_loop(0, count, one, 0)

    def end(s, carry):
        stores(s, wait)
        return carry

    lax.fori_loop(0, count, end, 0)


def finish(low, high, sending, plan, x, t, gain, before, integral, own, across, down, occ, done):
    pairs, _, nv, _ = x.shape
    half = pairs // 2
    operands = [plan, gain, occ, across, down, x, before, integral, own, t]
    in_specs = [SMEM] * 3 + [VMEM] * 2 + [ANY] * 5
    out_shape = [jax.ShapeDtypeStruct((pairs, nv, nv), f32)]
    if sending:
        out_shape += send_shapes(half, nv, 1)
    aliases = {}
    if done is not None:
        aliases = {len(operands) + k: k for k in range(len(done))}
        in_specs += [ANY] * len(done)
        operands += done
    two = pltpu.VMEM((2, nv, nv), f32)
    return pl.pallas_call(
        functools.partial(finish_kernel, low, high, sending),
        out_shape=out_shape,
        in_specs=in_specs,
        out_specs=[ANY] * len(out_shape),
        scratch_shapes=[
            two,
            pltpu.VMEM((high - low, nv, nv), f32),
            two,
            two,
            two,
            pltpu.VMEM((pairs, nv, nv), f32),
            pltpu.SemaphoreType.DMA((2, 4)),
            pltpu.SemaphoreType.DMA((high - low,)),
            pltpu.SemaphoreType.DMA((pairs,)),
            pltpu.SemaphoreType.DMA((half,)),
        ],
        input_output_aliases=aliases,
        compiler_params=PARAMS,
        cost_estimate=cost(2 * (high - low) * 12 * nv**3, 2 * (high - low) * nv * nv * 24),
        name="finish",
    )(*operands)


def integrals_kernel(early, groups, plan, slabs, *rest):
    rest, (left_buf, high, low, right_buf, out_buf, left_sem, right_sem, out_sem) = rest[:-8], rest[-8:]
    out = rest[-1]
    orbitals, nv, nq = slabs.shape
    pairs = out.shape[0]
    sources, used = [], 0
    for k, pieces in enumerate(groups):
        sources.append((plan[COLUMN * pairs + (2 if early else 4) + k], rest[used : used + pieces]))
        used += pieces
    count = plan[EARLY_COUNT * pairs] if early else pairs - plan[EARLY_COUNT * pairs]
    first = 0 if early else plan[EARLY_COUNT * pairs]
    pair = lambda s: plan[EARLY * pairs + first + s]

    def fetch(s, slot):
        right = plan[RIGHT * pairs + pair(s)]
        for base, pieces in sources:
            for o in range(orbitals):

                @pl.when(right == base + o)
                def _():
                    at = 0
                    for piece in pieces:
                        target = right_buf.at[slot, pl.ds(at, piece.shape[1])]
                        pltpu.make_async_copy(piece.at[o], target, right_sem.at[slot]).start()
                        at += piece.shape[1]

    def arrived(slot):
        pltpu.make_async_copy(slabs.at[0], right_buf.at[slot], right_sem.at[slot]).wait()

    def store(s, slot):
        return pltpu.make_async_copy(out_buf.at[slot], out.at[pair(s)], out_sem.at[slot])

    lefts = [pltpu.make_async_copy(slabs.at[o], left_buf.at[o], left_sem.at[o]) for o in range(orbitals)]
    for copy in lefts:
        copy.start()

    @pl.when(count > 0)
    def _():
        fetch(0, 0)

    for o in range(orbitals):
        lefts[o].wait()
        high[o], low[o] = split(left_buf[o])

    def one(s, carry):
        slot = s % 2

        @pl.when(s + 1 < count)
        def _():
            fetch(s + 1, 1 - slot)

        arrived(slot)

        @pl.when(s >= 2)
        def _():
            store(s - 2, slot).wait()

        left = plan[LEFT * pairs + pair(s)]
        rh, rl = split(right_buf[slot])
        wide = dot_nt(high[left], jnp.concatenate([rh, rl], axis=0))
        out_buf[slot] = wide[:, :nv] + wide[:, nv:] + dot_nt(low[left], rh)
        store(s, slot).start()
        return carry

    lax.fori_loop(0, count, one, 0)

    @pl.when(count >= 2)
    def _():
        store(count - 2, count % 2).wait()

    @pl.when(count >= 1)
    def _():
        store(count - 1, (count + 1) % 2).wait()


def pair_integrals(early, plan, slabs, pairs, groups, done=None):
    orbitals, nv, nq = slabs.shape
    operands = [plan, slabs]
    for group in groups:
        operands += group
    in_specs = [SMEM] + [ANY] * (len(operands) - 1)
    aliases = {}
    if done is not None:
        aliases = {len(operands): 0}
        operands.append(done)
        in_specs.append(ANY)
    return pl.pallas_call(
        functools.partial(integrals_kernel, early, [len(group) for group in groups]),
        out_shape=jax.ShapeDtypeStruct((pairs, nv, nv), f32),
        in_specs=in_specs,
        out_specs=ANY,
        scratch_shapes=[
            pltpu.VMEM((orbitals, nv, nq), f32),
            pltpu.VMEM((orbitals, nv, nq), bf16),
            pltpu.VMEM((orbitals, nv, nq), bf16),
            pltpu.VMEM((2, nv, nq), f32),
            pltpu.VMEM((2, nv, nv), f32),
            pltpu.SemaphoreType.DMA((orbitals,)),
            pltpu.SemaphoreType.DMA((2,)),
            pltpu.SemaphoreType.DMA((2,)),
        ],
        input_output_aliases=aliases,
        compiler_params=PARAMS,
        cost_estimate=cost(pairs * 3 * nv * nv * nq, pairs * 2 * nv * nq),
        name="pair_integrals",
    )(*operands)


def shards(slabs, amplitudes, intersections, fock_coupling, virt_energy, occ_pair_energy, pair_orbs, couplings):
    axis = "orb"
    count = lax.axis_size(axis)
    device = lax.axis_index(axis)
    selects_near = device % 2 == (device // 2) % 2
    orbitals, nv, nq = slabs.shape
    pairs = amplitudes.shape[0]
    half = pairs // 2

    everyone = range(count)
    chip_odd = lambda i: (i // 2) % 2
    inside = [(i, i ^ 1) for i in everyone]
    beside = [(i, (i + 1) % count if i % 2 else (i - 1) % count) for i in everyone]
    near_perm = [(i, i ^ 2) for i in everyone]
    far_perm = [(i, (i - 4 if chip_odd(i) else i + 4) % count) for i in everyone]
    send = lambda value, perm: lax.ppermute(value, axis, perm)

    lists_cross = send(couplings, beside)
    rows = nv // CHUNKS
    pieces = [slabs[:, k * rows : (k + 1) * rows] for k in range(CHUNKS)]
    *pieces, lists_cross = lax.optimization_barrier((*pieces, lists_cross))
    near = [send(piece, near_perm) for piece in pieces]
    intra_t = send(amplitudes, inside)
    slabs_swapped = send(slabs, inside)

    core = device % 2
    partner = device + 1 - 2 * core
    intra_list = jnp.where(core == 0, couplings[:, 1], couplings[:, 0])
    coupled_rows = jnp.concatenate(
        [couplings[:, 2] - device * pairs, intra_list - partner * pairs, jnp.stack([2 + 0 * core, 1 - core])]
    )

    partial = couple(0, 0, pairs, after(coupled_rows, *pieces), intersections, amplitudes, fock_coupling)
    near[0], partial = lax.optimization_barrier((near[0], partial))
    far = [send(near[0], far_perm)]
    partial = couple(1, 0, pairs, coupled_rows, intersections, intra_t, fock_coupling, partial, True)
    near[1], partial = lax.optimization_barrier((near[1], partial))
    far.append(send(near[1], far_perm))

    where = after(device.astype(jnp.int32).reshape(1), near[1])
    plan = make_plan(count, orbitals, where, couplings, lists_cross, pair_orbs)
    across, down = virt_energy, virt_energy.T
    cross_out = gather_rows(plan, amplitudes)
    near[2], far[0], plan, *cross_out = lax.optimization_barrier((near[2], far[0], plan, *cross_out))
    far.append(send(near[2], far_perm))
    chosen = jnp.where(selects_near, near[0], far[0])
    chosen, *cross_out = lax.optimization_barrier((chosen, *cross_out))
    cross_t = [send(rows_out, beside) for rows_out in cross_out]
    integrals = pair_integrals(True, plan, slabs, pairs, [[slabs_swapped], near])
    far[2], integrals = lax.optimization_barrier((far[2], integrals))
    relayed = [send(chosen, inside)] + [send(jnp.where(selects_near, n, f), inside) for n, f in zip(near[1:], far[1:])]
    integrals = pair_integrals(False, plan, slabs, pairs, [far, relayed], integrals)

    current = amplitudes
    for iteration in range(ITERS):
        if iteration > 0:
            cross_t = [send(rows_out, beside) for rows_out in cross_out]
            intra_t = send(current, inside)
            partial = couple(0, 0, pairs, coupled_rows, intersections, current, fock_coupling)
            partial = couple(1, 0, pairs, coupled_rows, intersections, intra_t, fock_coupling, partial, True)
        sending = iteration + 1 < ITERS
        done = None
        groups = list(enumerate(rank_groups(half, iteration)))
        for k, (low, high) in groups if iteration > 0 else groups[::-1]:
            done = finish(
                low,
                high,
                sending,
                plan,
                intersections,
                cross_t[k],
                fock_coupling,
                partial,
                integrals,
                current,
                across,
                down,
                occ_pair_energy,
                done,
            )
        current = done[0]
        if sending:
            cross_out = done[1:]
    return current


def solution(mesh):
    in_specs = (
        P("orb", None, None),
        P("orb", None, None),
        P("orb", None, None, None),
        P("orb", None),
        P("orb", None),
        P("orb"),
        P("orb", None),
        P("orb", None),
    )
    out_specs = P("orb", None, None)
    return jax.shard_map(shards, mesh=mesh, in_specs=in_specs, out_specs=out_specs, check_vma=False)
```
